32 devices in a mesh: rep: 2 (over x), grp: 16 (over z, y, core).
Axes of the slice: x: 2, y: 2, z: 4, core: 2. Of those that a mesh axis runs over, the one named last changes fastest.
Arguments:
- features: bfloat16 [8192, 128], P('grp'), may hold values from -6 to 6
- weight: bfloat16 [128, 256], replicated, may hold values from -0.5 to 0.5
- bias_row: float32 [256], replicated, may hold values from -3 to 3
- cotangent: bfloat16 [8192, 256], P('grp'), may hold values from -6 to 6
- tile_vals: bfloat16 [2, 16, 8, 12, 128, 128], P('rep', 'grp'), may hold values from -0.1875 to 0.1875
- row_block: int32 [2, 16, 8, 12], P('rep', 'grp'), may hold values from 0 to 3
- col_block: int32 [2, 16, 8, 12], P('rep', 'grp'), may hold values from 0 to 3
- counts: int32 [2, 16, 8], P('rep', 'grp'), may hold values from 1 to 12, as said below
- owner_map: int32 [16], replicated, may hold values from 0 to 15, each once
Outputs:
- hidden: bfloat16 [8192, 256], P('grp')
- grad_w: float32 [128, 256], replicated
- grad_x: float32 [8192, 128], P('grp')
The draws below stay inside these ranges and needn't reach their ends.
Inputs may be any that keep to these rules, and one draw needn't show every extreme that they name: `counts`: live slots of one device in one section; the most, 12, is reached in every draw. `owner_map`: each index of grp appears once; entries r * 8 to (r + 1) * 8 - 1 are the owners, in section order, whose column blocks replica group r holds.
All inputs are finite; a program needn't handle non-finite values.
Results may differ from the reference program's by a relative error of at most 0.0054.
Values may be sent and summed in bfloat16 or wider, within the bound.
A program may use at most 64 MiB of HBM per device.

```python
import jax
import jax.numpy as jnp
from jax import lax

D_IN = 128
HID = 256
TILE = 128
BLOCKS = 4
SLOTS = 12
SECTIONS = 8
NODES = 8192
N_REP = 2
N_GRP = 16


def draw_counts(key, part):
    key = jax.random.fold_in(key, 11)
    key_level, key_base, key_place = jax.random.split(key, 3)
    level = jax.random.randint(key_level, (N_REP, N_GRP, 1), 1, 5)
    base = jax.random.randint(key_base, (N_REP, N_GRP, SECTIONS), 0, SLOTS)
    filled = 1 + base * level // 4
    place = jax.random.randint(key_place, (), 0, N_REP * N_GRP * SECTIONS)
    flat = filled.reshape(-1)
    flat = jnp.where(jnp.arange(N_REP * N_GRP * SECTIONS) == place, SLOTS, flat)
    return flat.reshape(N_REP, N_GRP, SECTIONS).astype(jnp.int32)


def plant(array, rng, low, high):
    dims = array.shape
    spot = [jax.random.randint(jax.random.fold_in(rng, axis), (), 0, dims[axis]) for axis in range(len(dims))]
    array = array.at[tuple(spot)].set(low)
    longest = dims.index(max(dims))
    spot[longest] = (spot[longest] + 1) % dims[longest]
    return array.at[tuple(spot)].set(high)


def level_of(rng, shape, cuts, smallest, high):
    def one(axis_at, parts):
        steps = jax.random.uniform(jax.random.fold_in(jax.random.fold_in(rng, 6), axis_at), (parts,), jnp.float32, smallest / len(cuts), high / len(cuts))
        return jnp.repeat(jnp.exp(steps), shape[axis_at] // parts).reshape((-1,) + (1,) * (len(shape) - axis_at - 1))

    loudness = one(*cuts[0])
    for cut in cuts[1:]:
        loudness = loudness * one(*cut)
    return loudness


def gaussian(stream_key, shape, deviation, most, cuts=(), kind=jnp.bfloat16):
    drawn = jax.random.normal(stream_key, shape, jnp.float32) * deviation
    if len(cuts) > 0:
        drawn = level_of(stream_key, shape, cuts, -0.22, 0.18) * drawn
    return jnp.clip(drawn, min=-most, max=most).astype(kind)


def setup_inputs(seed: int = 0) -> dict:
    splits = jax.random.split(jax.random.key(seed), 10)
    features = gaussian(splits[0], (NODES, D_IN), 1.0, 6.0, ((0, 16),))
    weight = gaussian(splits[1], (D_IN, HID), D_IN ** -0.5, 0.5)
    bias_row = gaussian(splits[2], (HID,), 0.5, 3.0, (), jnp.float32)
    cotangent = gaussian(splits[3], (NODES, HID), 1.0, 6.0, ((0, 16),))
    tile_vals = gaussian(splits[4], (N_REP, N_GRP, SECTIONS, SLOTS, TILE, TILE), ((TILE * N_REP * 2 * SLOTS) ** -0.5), 0.1875, ((0, 2), (1, 16)))
    row_block = plant(jax.random.randint(splits[5], (N_REP, N_GRP, SECTIONS, SLOTS), 0, BLOCKS), jax.random.fold_in(splits[5], 1), 0, BLOCKS - 1).astype(jnp.int32)
    col_block = plant(jax.random.randint(splits[6], (N_REP, N_GRP, SECTIONS, SLOTS), 0, BLOCKS), jax.random.fold_in(splits[6], 1), 0, BLOCKS - 1).astype(jnp.int32)
    counts = draw_counts(jax.random.fold_in(splits[9], 71), 0)
    owner_map = jax.random.permutation(splits[8], N_GRP).astype(jnp.int32)
    return {"features": features, "weight": weight, "bias_row": bias_row, "cotangent": cotangent, "tile_vals": tile_vals, "row_block": row_block, "col_block": col_block, "counts": counts, "owner_map": owner_map}


def reference(features, weight, bias_row, cotangent, tile_vals, row_block, col_block, counts, owner_map):
    n_blocks = NODES // TILE
    owners = owner_map.reshape(N_REP, SECTIONS)
    slot_ids = jnp.arange(SLOTS, dtype=jnp.int32)
    dev_ids = jnp.arange(N_REP * N_GRP, dtype=jnp.int32)

    def tile_lists(dev_index):
        rep_pos = dev_index // N_GRP
        grp_pos = dev_index % N_GRP
        live_slot = (slot_ids[None, :] < counts[rep_pos, grp_pos][:, None]).astype(jnp.float32)
        rows_at = (grp_pos * BLOCKS + row_block[rep_pos, grp_pos]).reshape(-1).astype(jnp.int32)
        cols_at = (owners[rep_pos][:, None] * BLOCKS + col_block[rep_pos, grp_pos]).reshape(-1).astype(jnp.int32)
        values = tile_vals[rep_pos, grp_pos].reshape(-1, TILE, TILE).astype(jnp.float32)
        values = values * live_slot.reshape(-1, 1, 1)
        return values, rows_at, cols_at

    feat_blocks = features.astype(jnp.float32).reshape(n_blocks, TILE, D_IN)

    def forward_step(agg_total, dev_index):
        values, rows_at, cols_at = tile_lists(dev_index)
        product = jnp.einsum("kij,kjd->kid", values, feat_blocks[cols_at])
        return agg_total.at[rows_at].add(product), None

    agg_total, _ = lax.scan(forward_step, jnp.zeros((n_blocks, TILE, D_IN), jnp.float32), dev_ids)
    aggregated = agg_total.reshape(NODES, D_IN) + features.astype(jnp.float32)
    agg_rows = aggregated.astype(jnp.bfloat16)
    pre_act = jnp.dot(agg_rows, weight, preferred_element_type=jnp.float32) + bias_row
    hidden = jax.nn.silu(pre_act).astype(jnp.bfloat16)
    sigmoid_val = jax.nn.sigmoid(pre_act)
    grad_pre = (cotangent.astype(jnp.float32) * sigmoid_val * (1.0 + pre_act * (1.0 - sigmoid_val))).astype(jnp.bfloat16)
    grad_w = jnp.dot(agg_rows.T, grad_pre, preferred_element_type=jnp.float32) * (NODES ** -0.5)
    back_rows = jnp.dot(grad_pre, weight.T, preferred_element_type=jnp.float32).astype(jnp.bfloat16)
    back_blocks = back_rows.astype(jnp.float32).reshape(n_blocks, TILE, D_IN)

    def backward_step(trans_total, dev_index):
        values, rows_at, cols_at = tile_lists(dev_index)
        product = jnp.einsum("kji,kjd->kid", values, back_blocks[rows_at])
        return trans_total.at[cols_at].add(product), None

    trans_total, _ = lax.scan(backward_step, jnp.zeros((n_blocks, TILE, D_IN), jnp.float32), dev_ids)
    grad_x = trans_total.reshape(NODES, D_IN) + back_rows.astype(jnp.float32)
    return hidden, grad_w, grad_x
```

```python
import functools

import jax
import jax.numpy as jnp
from jax import lax
from jax.experimental import pallas as pl
from jax.experimental.pallas import tpu as pltpu
from jax.sharding import PartitionSpec as P

BF16 = jnp.bfloat16
F32 = jnp.float32


def build_kernel(row_ref, col_ref, count_ref, tiles_ref, out_ref, acc):
    s = pl.program_id(0)
    side = tiles_ref.shape[-1]
    acc[...] = jnp.zeros_like(acc)

    def add(k, carry):
        rows = pl.ds(pl.multiple_of(row_ref[0, 0, s, k] * side, side), side)
        c = col_ref[0, 0, s, k]
        acc[c, rows, :] += tiles_ref[0, 0, 0, k].astype(F32)
        return carry

    lax.fori_loop(0, count_ref[0, 0, s], add, 0)
    for c in range(acc.shape[0]):
        out_ref[0, :, c * side : (c + 1) * side] = acc[c].astype(BF16)


def build_adjacency(tile_vals, row_block, col_block, counts, n_blocks):
    _, _, n_sections, n_slots, side, _ = tile_vals.shape
    rows = n_blocks * side
    return pl.pallas_call(
        build_kernel,
        out_shape=jax.ShapeDtypeStruct((n_sections, rows, rows), BF16),
        grid_spec=pltpu.PrefetchScalarGridSpec(
            num_scalar_prefetch=3,
            grid=(n_sections,),
            in_specs=[
                pl.BlockSpec((1, 1, 1, n_slots, side, side), lambda s, *_: (0, 0, s, 0, 0, 0))
            ],
            out_specs=pl.BlockSpec((1, rows, rows), lambda s, *_: (s, 0, 0)),
            scratch_shapes=[pltpu.VMEM((n_blocks, rows, side), F32)],
        ),
    )(row_block, col_block, counts, tile_vals)


def main_kernel(
    n_rep, n_z, n_y, n_c, scale,
    owner_ref, feat_ref, weight_ref, bias_ref, cot_ref, adj_ref,
    hidden_ref, gw_ref, gx_ref,
    adj, feats, part, rc, rza, rzb, rya, ryb, xg, xo, gwt, gwc, gwy, gwz, back_ref,
    adj_sem, ag_s, ag_r, sib_s, sib_r, rc_s, rc_r, rs_s, rs_r, x_s, x_r, gw_s, gw_r, gwz_s, gwz_r, gwx_s, gwx_r,
):
    rep = lax.axis_index("rep")
    me = lax.axis_index("grp")
    z = me // (n_y * n_c)
    y = (me // n_c) % n_y
    c = me % n_c
    half = feat_ref.shape[0] // 2
    n_sections = adj_ref.shape[0]
    ROWS_A, ROWS_B = pl.ds(0, half), pl.ds(half, half)

    def dev(zz, yy, cc):
        return (rep, (zz * n_y + yy) * n_c + cc)

    def rcopy(src, dst, s_sem, r_sem, target):
        return pltpu.make_async_remote_copy(
            src_ref=src, dst_ref=dst, send_sem=s_sem, recv_sem=r_sem,
            device_id=target, device_id_type=pl.DeviceIdType.MESH,
        )

    adj_copy = pltpu.make_async_copy(adj_ref, adj.at[pl.ds(0, n_sections)], adj_sem)
    adj_copy.start()

    barrier = pltpu.get_barrier_semaphore()

    def greet(target):
        pl.semaphore_signal(barrier, inc=1, device_id=target, device_id_type=pl.DeviceIdType.MESH)

    greet(dev(z, y, 1 - c))
    greet(dev(z, 1 - y, c))
    for j in range(1, n_z):
        greet(dev((z + j) % n_z, y, c))
    for j in range(1, n_rep):
        greet(((rep + j) % n_rep, me))
    feats[z, y, c] = feat_ref[...]
    adj[n_sections] = jnp.zeros_like(adj[n_sections])
    pl.semaphore_wait(barrier, 2 + n_z - 1 + n_rep - 1)

    def a_z(d, t):
        src = z - t if d == 0 else z + t
        blk = feats.at[src, :, c, ROWS_A]
        return rcopy(blk, blk, ag_s.at[0, d, t], ag_r.at[0, d, t], dev(z + 1 if d == 0 else z - 1, y, c))

    def b_z(d, t):
        src = z - t if d == 0 else z + t
        blk = feats.at[src, y, c, ROWS_B]
        return rcopy(blk, blk, ag_s.at[1, d, t], ag_r.at[1, d, t], dev(z + 1 if d == 0 else z - 1, y, c))

    def send_ok(d, t):
        return (z - t >= 0) & (z + 1 < n_z) if d == 0 else (z + t < n_z) & (z >= 1)

    def recv_ok(d, t):
        return z - 1 - t >= 0 if d == 0 else z + 1 + t < n_z

    def origin(d, t):
        return z - 1 - t if d == 0 else z + 1 + t

    def arrived(kind, d, t):
        src = origin(d, t)
        blk = feats.at[src, :, c, ROWS_A] if kind == 0 else feats.at[src, y, c, ROWS_B]
        if kind == 2:
            blk = feats.at[src, 1 - y, c, ROWS_B]
        return rcopy(blk, blk, ag_s.at[kind, d, t], ag_r.at[kind, d, t], dev(z, y, 1 - c))

    def b_y(d, t):
        src = origin(d, t)
        blk = feats.at[src, y, c, ROWS_B]
        return rcopy(blk, blk, ag_s.at[2, d, t], ag_r.at[2, d, t], dev(z, 1 - y, c))

    def sib(kind, src, i, got=False):
        blk = feats.at[src, :, 1 - c if got else c, ROWS_A if kind == 0 else ROWS_B]
        return rcopy(blk, blk, sib_s.at[kind, i], sib_r.at[kind, i], dev(z, y, 1 - c))

    def own_y(rows, i, got=False):
        blk = feats.at[z, 1 - y if got else y, c, rows]
        return rcopy(blk, blk, ag_s.at[3, i, 0], ag_r.at[3, i, 0], dev(z, 1 - y, c))

    own_y(ROWS_A, 0).start()
    for d in range(2):
        pl.when(send_ok(d, 0))(b_z(d, 0).start)
    own_y(ROWS_B, 1).start()
    own_y(ROWS_A, 0, True).wait_recv()
    for d in range(2):
        pl.when(send_ok(d, 0))(a_z(d, 0).start)
    sib(0, z, 0).start()
    own_y(ROWS_B, 1, True).wait_recv()
    sib(1, z, 0).start()
    for t in range(n_z - 1):
        for d in range(2):
            pl.when(recv_ok(d, t))(arrived(1, d, t).wait_recv)
            if t + 1 < n_z - 1:
                pl.when(send_ok(d, t + 1))(b_z(d, t + 1).start)
            pl.when(recv_ok(d, t))(b_y(d, t).start)
        for d in range(2):
            pl.when(recv_ok(d, t))(arrived(0, d, t).wait_recv)
            if t + 1 < n_z - 1:
                pl.when(send_ok(d, t + 1))(a_z(d, t + 1).start)
            pl.when(recv_ok(d, t))(sib(0, origin(d, t), 1 + 2 * t + d).start)
        for d in range(2):
            pl.when(recv_ok(d, t))(arrived(2, d, t).wait_recv)
            pl.when(recv_ok(d, t))(sib(1, origin(d, t), 1 + 2 * t + d).start)
    for kind in range(2):
        sib(kind, z, 0, True).wait_recv()
    for t in range(n_z - 1):
        for d in range(2):
            for kind in range(2):
                pl.when(recv_ok(d, t))(sib(kind, origin(d, t), 1 + 2 * t + d, True).wait_recv)
    adj_copy.wait()

    def forward(s, total):
        o = owner_ref[rep * n_sections + s]
        f = feats[lax.div(o, n_y * n_c), lax.rem(lax.div(o, n_c), n_y), lax.rem(o, n_c)]
        return total + jnp.dot(adj[s], f, preferred_element_type=F32)

    total = lax.fori_loop(0, n_sections, forward, jnp.zeros(feat_ref.shape, F32))
    xg[rep] = total.astype(BF16)

    def x_copy(buf, kind, j, got=False):
        other = (rep + n_rep - j if got else rep + j) % n_rep
        blk = buf.at[other if got else rep]
        return rcopy(blk, blk, x_s.at[kind, j - 1], x_r.at[kind, j - 1], (other, me))

    for j in range(1, n_rep):
        x_copy(xg, 0, j).start()
    for j in range(1, n_rep):
        x_copy(xg, 0, j, True).wait_recv()
    agg = feat_ref[...].astype(F32)
    for r in range(n_rep):
        agg = agg + xg[r].astype(F32)
    agg_rows = agg.astype(BF16)
    pre = jnp.dot(agg_rows, weight_ref[...], preferred_element_type=F32) + bias_ref[...]
    sig = jax.nn.sigmoid(pre)
    hidden_ref[...] = (pre * sig).astype(BF16)
    grad_pre = (cot_ref[...].astype(F32) * sig * (1.0 + pre * (1.0 - sig))).astype(BF16)
    back = lax.dot_general(
        grad_pre, weight_ref[...], (((1,), (1,)), ((), ())), preferred_element_type=F32
    ).astype(BF16)
    back_ref[...] = back
    gwt[...] = lax.dot_general(agg_rows, grad_pre, (((0,), (0,)), ((), ())), preferred_element_type=F32)

    g_rows = gw_ref.shape[0] // (n_rep * n_c)
    g_cols = gw_ref.shape[1] // n_y

    def g_row(r, cc):
        return pl.ds(pl.multiple_of((r * n_c + cc) * g_rows, g_rows), g_rows)

    def g_col(yy):
        return pl.ds(pl.multiple_of(yy * g_cols, g_cols), g_cols)

    gw_c = rcopy(gwt.at[g_row(rep, 1 - c)], gwc, gw_s.at[0], gw_r.at[0], dev(z, y, 1 - c))
    gw_c.start()

    def rc_copy(d):
        return rcopy(part.at[d, :, 1 - c], rc.at[d], rc_s.at[d], rc_r.at[d], dev(z, y, 1 - c))

    def transposed(d, carry):
        for yy in range(n_y):
            for cc in range(n_c):
                m = (d * n_y + yy) * n_c + cc
                idx = jnp.int32(n_sections)
                for s in range(n_sections):
                    idx = jnp.where(owner_ref[rep * n_sections + s] == m, s, idx)
                part[d, yy, cc] = lax.dot_general(
                    adj[idx], back_ref[...], (((0,), (0,)), ((), ())), preferred_element_type=F32
                ).astype(BF16)
        rc_copy(d).start()
        return carry

    lax.fori_loop(0, n_z, transposed, 0)

    gw_c.wait_recv()
    gwc[...] += gwt[g_row(rep, c), :]
    gw_y = rcopy(gwc.at[:, g_col(1 - y)], gwy, gw_s.at[1], gw_r.at[1], dev(z, 1 - y, c))
    gw_y.start()

    def add_core(d, carry):
        rc_copy(d).wait_recv()
        for yy in range(n_y):
            part[d, yy, c] = (part[d, yy, c].astype(F32) + rc[d, yy].astype(F32)).astype(BF16)
        return carry

    def yb_copy(d):
        return rcopy(part.at[d, 1 - y, c, ROWS_B], ryb.at[d], rs_s.at[3, 0, d], rs_r.at[3, 0, d], dev(z, 1 - y, c))

    def add_core_send(d, carry):
        add_core(d, carry)
        yb_copy(d).start()
        return carry

    lax.fori_loop(0, n_z, add_core_send, 0)

    def rs_dest(d, t):
        return z - n_z + 1 + t if d == 0 else z + n_z - 1 - t

    def rs_send_ok(d, t):
        return z - n_z + 1 + t >= 0 if d == 0 else z + n_z - 1 - t <= n_z - 1

    def rs_send_ok2(d, t):
        dst = rs_dest(d, t)
        return (dst >= 0) & (z >= 1) if d == 0 else (dst <= n_z - 1) & (z <= n_z - 2)

    def rs_recv_ok(d, t):
        w = z + 1 if d == 0 else z - 1
        dst = w - n_z + 1 + t if d == 0 else w + n_z - 1 - t
        return (w <= n_z - 1) & (dst >= 0) if d == 0 else (w >= 0) & (dst <= n_z - 1)

    def rs_recv_dest(d, t):
        return z + 2 - n_z + t if d == 0 else z + n_z - 2 - t

    def za_copy(d, t):
        return rcopy(
            part.at[rs_dest(d, t), :, c, ROWS_A], rza.at[d, t],
            rs_s.at[0, d, t], rs_r.at[0, d, t], dev(z - 1 if d == 0 else z + 1, y, c),
        )

    def zb_copy(d, t):
        return rcopy(
            part.at[rs_dest(d, t), y, c, ROWS_B], rzb.at[d, t],
            rs_s.at[1, d, t], rs_r.at[1, d, t], dev(z - 1 if d == 0 else z + 1, y, c),
        )

    def za_got(d, t):
        return rcopy(
            part.at[z, :, c, ROWS_A], rza.at[d, t],
            rs_s.at[0, d, t], rs_r.at[0, d, t], dev(z, y, 1 - c),
        )

    def zb_got(d, t):
        return rcopy(
            part.at[z, y, c, ROWS_B], rzb.at[d, t],
            rs_s.at[1, d, t], rs_r.at[1, d, t], dev(z, y, 1 - c),
        )

    def take_a(d, t):
        za_got(d, t).wait_recv()
        dst = rs_recv_dest(d, t)
        for yy in range(n_y):
            part[dst, yy, c, ROWS_A] = (
                part[dst, yy, c, ROWS_A].astype(F32) + rza[d, t, yy].astype(F32)
            ).astype(BF16)

    def take_b(d, t):
        zb_got(d, t).wait_recv()
        dst = rs_recv_dest(d, t)
        part[dst, y, c, ROWS_B] = (
            part[dst, y, c, ROWS_B].astype(F32) + rzb[d, t].astype(F32)
        ).astype(BF16)

    for d in range(2):
        pl.when(rs_send_ok2(d, 0))(za_copy(d, 0).start)

    gw_y.wait_recv()
    gwz[z] = gwc[:, g_col(y)] + gwy[...]

    def gz_copy(j, got=False):
        other = (z + n_z - j if got else z + j) % n_z
        blk = gwz.at[other if got else z]
        return rcopy(blk, blk, gwz_s.at[j - 1], gwz_r.at[j - 1], dev(other, y, c))

    for j in range(1, n_z):
        gz_copy(j).start()

    def take_yb(d, carry):
        yb_copy(d).wait_recv()
        part[d, y, c, ROWS_B] = (
            part[d, y, c, ROWS_B].astype(F32) + ryb[d].astype(F32)
        ).astype(BF16)
        return carry

    lax.fori_loop(0, n_z, take_yb, 0)
    for t in range(n_z - 1):
        for d in range(2):
            pl.when(rs_send_ok2(d, t))(zb_copy(d, t).start)
        for d in range(2):
            pl.when(rs_recv_ok(d, t))(functools.partial(take_a, d, t))
            if t + 1 < n_z - 1:
                pl.when(rs_send_ok2(d, t + 1))(za_copy(d, t + 1).start)
        for d in range(2):
            pl.when(rs_recv_ok(d, t))(functools.partial(take_b, d, t))
    ya = rcopy(part.at[z, 1 - y, c, ROWS_A], rya, rs_s.at[2, 0, 0], rs_r.at[2, 0, 0], dev(z, 1 - y, c))
    ya.start()

    for j in range(1, n_z):
        gz_copy(j, True).wait_recv()
    gsum = gwz[0]
    for j in range(1, n_z):
        gsum = gsum + gwz[j]
    gw_ref[g_row(rep, c), g_col(y)] = gsum * scale
    mine = gw_ref.at[g_row(rep, c), g_col(y)]
    g_y = rcopy(mine, mine, gw_s.at[2], gw_r.at[2], dev(z, 1 - y, c))
    g_y.start()

    ya.wait_recv()
    xo[rep, ROWS_B] = part[z, y, c, ROWS_B]
    xo[rep, ROWS_A] = (part[z, y, c, ROWS_A].astype(F32) + rya[...].astype(F32)).astype(BF16)
    for j in range(1, n_rep):
        x_copy(xo, 1, j).start()

    theirs = gw_ref.at[g_row(rep, c), g_col(1 - y)]
    rcopy(theirs, theirs, gw_s.at[2], gw_r.at[2], dev(z, 1 - y, c)).wait_recv()
    strip = gw_ref.at[g_row(rep, c)]
    g_c = rcopy(strip, strip, gw_s.at[3], gw_r.at[3], dev(z, y, 1 - c))
    g_c.start()
    strip2 = gw_ref.at[g_row(rep, 1 - c)]
    rcopy(strip2, strip2, gw_s.at[3], gw_r.at[3], dev(z, y, 1 - c)).wait_recv()

    def gx_copy(j, got=False):
        other = (rep + n_rep - j if got else rep + j) % n_rep
        rows = gw_ref.shape[0] // n_rep
        blk = gw_ref.at[pl.ds(pl.multiple_of((other if got else rep) * rows, rows), rows)]
        return rcopy(blk, blk, gwx_s.at[j - 1], gwx_r.at[j - 1], (other, me))

    for j in range(1, n_rep):
        gx_copy(j).start()
    for j in range(1, n_rep):
        x_copy(xo, 1, j, True).wait_recv()
    out = back_ref[...].astype(F32)
    for r in range(n_rep):
        out = out + xo[r].astype(F32)
    gx_ref[...] = out
    for j in range(1, n_rep):
        gx_copy(j, True).wait_recv()

    own_y(ROWS_A, 0).wait_send()
    own_y(ROWS_B, 1).wait_send()
    for kind in range(2):
        sib(kind, z, 0).wait_send()
    for t in range(n_z - 1):
        for d in range(2):
            pl.when(send_ok(d, t))(a_z(d, t).wait_send)
            pl.when(send_ok(d, t))(b_z(d, t).wait_send)
            pl.when(recv_ok(d, t))(b_y(d, t).wait_send)
            for kind in range(2):
                pl.when(recv_ok(d, t))(sib(kind, origin(d, t), 1 + 2 * t + d).wait_send)
            pl.when(rs_send_ok2(d, t))(za_copy(d, t).wait_send)
            pl.when(rs_send_ok2(d, t))(zb_copy(d, t).wait_send)
    for d in range(n_z):
        rc_copy(d).wait_send()
        yb_copy(d).wait_send()
    ya.wait_send()
    for j in range(1, n_rep):
        x_copy(xg, 0, j).wait_send()
        x_copy(xo, 1, j).wait_send()
        gx_copy(j).wait_send()
    for j in range(1, n_z):
        gz_copy(j).wait_send()
    for g in (gw_c, gw_y, g_y, g_c):
        g.wait_send()


def per_device(
    n_rep, n_grp,
    features, weight, bias_row, cotangent, tile_vals, row_block, col_block, counts, owner_map
):
    side = tile_vals.shape[-1]
    n_sections = tile_vals.shape[2]
    rows, width = features.shape
    hid = weight.shape[1]
    n_c, n_y = 2, 2
    n_z = n_grp // (n_c * n_y)
    half = rows // 2
    adjacency = build_adjacency(tile_vals, row_block, col_block, counts, rows // side)
    vmem = pl.BlockSpec(memory_space=pltpu.VMEM)
    dma = pltpu.SemaphoreType.DMA
    g_rows = width // (n_rep * n_c)
    g_cols = hid // n_y
    return pl.pallas_call(
        functools.partial(main_kernel, n_rep, n_z, n_y, n_c, float((rows * n_grp) ** (-0.5))),
        out_shape=(
            jax.ShapeDtypeStruct((rows, hid), BF16),
            jax.ShapeDtypeStruct((width, hid), F32),
            jax.ShapeDtypeStruct((rows, width), F32),
        ),
        in_specs=[pl.BlockSpec(memory_space=pltpu.SMEM), vmem, vmem, vmem, vmem,
                  pl.BlockSpec(memory_space=pl.ANY)],
        out_specs=(vmem, vmem, vmem),
        scratch_shapes=[
            pltpu.VMEM((n_sections + 1, rows, rows), BF16),
            pltpu.VMEM((n_z, n_y, n_c, rows, width), BF16),
            pltpu.VMEM((n_z, n_y, n_c, rows, width), BF16),
            pltpu.VMEM((n_z, n_y, rows, width), BF16),
            pltpu.VMEM((2, n_z - 1, n_y, half, width), BF16),
            pltpu.VMEM((2, n_z - 1, half, width), BF16),
            pltpu.VMEM((half, width), BF16),
            pltpu.VMEM((n_z, half, width), BF16),
            pltpu.VMEM((n_rep, rows, width), BF16),
            pltpu.VMEM((n_rep, rows, width), BF16),
            pltpu.VMEM((width, hid), F32),
            pltpu.VMEM((g_rows, hid), F32),
            pltpu.VMEM((g_rows, g_cols), F32),
            pltpu.VMEM((n_z, g_rows, g_cols), F32),
            pltpu.VMEM((rows, width), BF16),
            dma,
            dma((4, 2, n_z)), dma((4, 2, n_z)),
            dma((2, 2 * n_z)), dma((2, 2 * n_z)),
            dma((n_z,)), dma((n_z,)),
            dma((4, 2, n_z)), dma((4, 2, n_z)),
            dma((2, n_rep)), dma((2, n_rep)),
            dma((4,)), dma((4,)),
            dma((n_z,)), dma((n_z,)),
            dma((n_rep,)), dma((n_rep,)),
        ],
        compiler_params=pltpu.CompilerParams(
            collective_id=0, has_side_effects=True, vmem_limit_bytes=56 * 1024 * 1024
        ),
    )(owner_map, features, weight, bias_row[None, :], cotangent, adjacency)


def solution(mesh):
    in_specs = (
        P("grp", None),
        P(),
        P(),
        P("grp", None),
        P("rep", "grp", None, None, None, None),
        P("rep", "grp", None, None),
        P("rep", "grp", None, None),
        P("rep", "grp", None),
        P(),
    )
    out_specs = (P("grp", None), P(), P("grp", None))
    return jax.shard_map(
        functools.partial(per_device, mesh.shape["rep"], mesh.shape["grp"]),
        mesh=mesh, in_specs=in_specs, out_specs=out_specs, check_vma=False,
    )
```

```python
import functools

import jax
import jax.numpy as jnp
from jax import lax
from jax.experimental import pallas as pl
from jax.experimental.pallas import tpu as pltpu
from jax.sharding import PartitionSpec as P

BF16 = jnp.bfloat16
F32 = jnp.float32


def main_kernel(
    n_rep, n_z, n_y, n_c, scale,
    owner_ref, row_ref, col_ref, count_ref, feat_hbm, weight_hbm, bias_ref, cot_hbm, tiles_hbm,
    hidden_hbm, gw_ref, gx_ref,
    tiles, feat_ref, weight_ref, cot_ref, hidden_ref, adj, feats, part, rc, rza, rzb, rya, ryb, xg, xo, gwt, gwc, gwy, gwz, back_ref,
    tile_sem, in_sem, ag_s, ag_r, sib_s, sib_r, rc_s, rc_r, rs_s, rs_r, x_s, x_r, gw_s, gw_r, gwz_s, gwz_r, gwx_s, gwx_r,
):
    rep = lax.axis_index("rep")
    me = lax.axis_index("grp")
    z = me // (n_y * n_c)
    y = (me // n_c) % n_y
    c = me % n_c
    half = feat_ref.shape[0] // 2
    n_sections, n_slots, side, _ = tiles.shape
    n_blocks = feat_ref.shape[0] // side
    ROWS_A, ROWS_B = pl.ds(0, half), pl.ds(half, half)

    def dev(zz, yy, cc):
        return (rep, (zz * n_y + yy) * n_c + cc)

    def rcopy(src, dst, s_sem, r_sem, target):
        return pltpu.make_async_remote_copy(
            src_ref=src, dst_ref=dst, send_sem=s_sem, recv_sem=r_sem,
            device_id=target, device_id_type=pl.DeviceIdType.MESH,
        )

    loads = [
        pltpu.make_async_copy(feat_hbm, feats.at[z, y, c], in_sem.at[0]),
        pltpu.make_async_copy(feat_hbm, feat_ref, in_sem.at[1]),
        pltpu.make_async_copy(weight_hbm, weight_ref, in_sem.at[2]),
        pltpu.make_async_copy(cot_hbm, cot_ref, in_sem.at[3]),
    ]
    loads[0].start()

    barrier = pltpu.get_barrier_semaphore()

    def greet(target):
        pl.semaphore_signal(barrier, inc=1, device_id=target, device_id_type=pl.DeviceIdType.MESH)

    greet(dev(z, y, 1 - c))
    greet(dev(z, 1 - y, c))
    for j in range(1, n_z):
        greet(dev((z + j) % n_z, y, c))
    for j in range(1, n_rep):
        greet(((rep + j) % n_rep, me))
    tile_loads = [
        pltpu.make_async_copy(tiles_hbm.at[0, 0, s], tiles.at[s], tile_sem.at[s])
        for s in range(n_sections)
    ]
    for s in range(n_sections):
        tile_loads[s].start()
    for load in loads[1:]:
        load.start()
    adj[n_sections] = jnp.zeros_like(adj[n_sections])
    pl.semaphore_wait(barrier, 2 + n_z - 1 + n_rep - 1)
    loads[0].wait()

    part_rows = side // 2

    def build(s):
        tile_loads[s].wait()
        place = [
            jnp.where(
                k < count_ref[0, 0, s], row_ref[0, 0, s, k] * n_blocks + col_ref[0, 0, s, k], -1
            )
            for k in range(n_slots)
        ]

        def column(j, carry):
            cols = pl.ds(pl.multiple_of(j * side, side), side)
            for h in range(2):
                sums = [jnp.zeros((part_rows, side), F32)] * n_blocks
                for k in range(n_slots):
                    tile = tiles[s, k, h * part_rows : (h + 1) * part_rows, :].astype(F32)
                    for i in range(n_blocks):
                        pick = jnp.where(place[k] == i * n_blocks + j, 1.0, 0.0).astype(F32)
                        sums[i] = sums[i] + pick * tile
                for i in range(n_blocks):
                    lo = i * side + h * part_rows
                    adj[s, lo : lo + part_rows, cols] = sums[i].astype(BF16)
            return carry

        lax.fori_loop(0, n_blocks, column, 0)

    todo = list(range(n_sections))

    def build_next():
        if todo:
            build(todo.pop(0))

    def a_z(d, t):
        src = z - t if d == 0 else z + t
        blk = feats.at[src, :, c, ROWS_A]
        return rcopy(blk, blk, ag_s.at[0, d, t], ag_r.at[0, d, t], dev(z + 1 if d == 0 else z - 1, y, c))

    def b_z(d, t):
        src = z - t if d == 0 else z + t
        blk = feats.at[src, y, c, ROWS_B]
        return rcopy(blk, blk, ag_s.at[1, d, t], ag_r.at[1, d, t], dev(z + 1 if d == 0 else z - 1, y, c))

    def send_ok(d, t):
        return (z - t >= 0) & (z + 1 < n_z) if d == 0 else (z + t < n_z) & (z >= 1)

    def recv_ok(d, t):
        return z - 1 - t >= 0 if d == 0 else z + 1 + t < n_z

    def origin(d, t):
        return z - 1 - t if d == 0 else z + 1 + t

    def arrived(kind, d, t):
        src = origin(d, t)
        blk = feats.at[src, :, c, ROWS_A] if kind == 0 else feats.at[src, y, c, ROWS_B]
        if kind == 2:
            blk = feats.at[src, 1 - y, c, ROWS_B]
        return rcopy(blk, blk, ag_s.at[kind, d, t], ag_r.at[kind, d, t], dev(z, y, 1 - c))

    def b_y(d, t):
        src = origin(d, t)
        blk = feats.at[src, y, c, ROWS_B]
        return rcopy(blk, blk, ag_s.at[2, d, t], ag_r.at[2, d, t], dev(z, 1 - y, c))

    def sib(kind, src, i, got=False):
        blk = feats.at[src, :, 1 - c if got else c, ROWS_A if kind == 0 else ROWS_B]
        return rcopy(blk, blk, sib_s.at[kind, i], sib_r.at[kind, i], dev(z, y, 1 - c))

    def own_y(rows, i, got=False):
        blk = feats.at[z, 1 - y if got else y, c, rows]
        return rcopy(blk, blk, ag_s.at[3, i, 0], ag_r.at[3, i, 0], dev(z, 1 - y, c))

    own_y(ROWS_A, 0).start()
    for d in range(2):
        pl.when(send_ok(d, 0))(b_z(d, 0).start)
    own_y(ROWS_B, 1).start()
    build_next()
    own_y(ROWS_A, 0, True).wait_recv()
    for d in range(2):
        pl.when(send_ok(d, 0))(a_z(d, 0).start)
    sib(0, z, 0).start()
    build_next()
    own_y(ROWS_B, 1, True).wait_recv()
    sib(1, z, 0).start()
    for t in range(n_z - 1):
        build_next()
        for d in range(2):
            pl.when(recv_ok(d, t))(arrived(1, d, t).wait_recv)
            if t + 1 < n_z - 1:
                pl.when(send_ok(d, t + 1))(b_z(d, t + 1).start)
            pl.when(recv_ok(d, t))(b_y(d, t).start)
        build_next()
        for d in range(2):
            pl.when(recv_ok(d, t))(arrived(0, d, t).wait_recv)
            if t + 1 < n_z - 1:
                pl.when(send_ok(d, t + 1))(a_z(d, t + 1).start)
            pl.when(recv_ok(d, t))(sib(0, origin(d, t), 1 + 2 * t + d).start)
        for d in range(2):
            pl.when(recv_ok(d, t))(arrived(2, d, t).wait_recv)
            pl.when(recv_ok(d, t))(sib(1, origin(d, t), 1 + 2 * t + d).start)
    while todo:
        build_next()
    for kind in range(2):
        sib(kind, z, 0, True).wait_recv()
    for t in range(n_z - 1):
        for d in range(2):
            for kind in range(2):
                pl.when(recv_ok(d, t))(sib(kind, origin(d, t), 1 + 2 * t + d, True).wait_recv)
    for load in loads[1:]:
        load.wait()

    def forward(s, total):
        o = owner_ref[rep * n_sections + s]
        f = feats[lax.div(o, n_y * n_c), lax.rem(lax.div(o, n_c), n_y), lax.rem(o, n_c)]
        return total + jnp.dot(adj[s], f, preferred_element_type=F32)

    total = lax.fori_loop(0, n_sections, forward, jnp.zeros(feat_ref.shape, F32))
    xg[rep] = total.astype(BF16)

    def x_copy(buf, kind, j, got=False):
        other = (rep + n_rep - j if got else rep + j) % n_rep
        blk = buf.at[other if got else rep]
        return rcopy(blk, blk, x_s.at[kind, j - 1], x_r.at[kind, j - 1], (other, me))

    for j in range(1, n_rep):
        x_copy(xg, 0, j).start()
    for j in range(1, n_rep):
        x_copy(xg, 0, j, True).wait_recv()
    agg = feat_ref[...].astype(F32)
    for r in range(n_rep):
        agg = agg + xg[r].astype(F32)
    agg_rows = agg.astype(BF16)
    pre = jnp.dot(agg_rows, weight_ref[...], preferred_element_type=F32) + bias_ref[...]
    sig = jax.nn.sigmoid(pre)
    hidden_ref[...] = (pre * sig).astype(BF16)
    store = pltpu.make_async_copy(hidden_ref, hidden_hbm, in_sem.at[0])
    store.start()
    grad_pre = (cot_ref[...].astype(F32) * sig * (1.0 + pre * (1.0 - sig))).astype(BF16)
    back = lax.dot_general(
        grad_pre, weight_ref[...], (((1,), (1,)), ((), ())), preferred_element_type=F32
    ).astype(BF16)
    back_ref[...] = back
    gwt[...] = lax.dot_general(agg_rows, grad_pre, (((0,), (0,)), ((), ())), preferred_element_type=F32)

    g_rows = gw_ref.shape[0] // (n_rep * n_c)
    g_cols = gw_ref.shape[1] // n_y

    def g_row(r, cc):
        return pl.ds(pl.multiple_of((r * n_c + cc) * g_rows, g_rows), g_rows)

    def g_col(yy):
        return pl.ds(pl.multiple_of(yy * g_cols, g_cols), g_cols)

    gw_c = rcopy(gwt.at[g_row(rep, 1 - c)], gwc, gw_s.at[0], gw_r.at[0], dev(z, y, 1 - c))
    gw_c.start()

    def rc_copy(d):
        return rcopy(part.at[d, :, 1 - c], rc.at[d], rc_s.at[d], rc_r.at[d], dev(z, y, 1 - c))

    def transposed(d, carry):
        for yy in range(n_y):
            for cc in range(n_c):
                m = (d * n_y + yy) * n_c + cc
                idx = jnp.int32(n_sections)
                for s in range(n_sections):
                    idx = jnp.where(owner_ref[rep * n_sections + s] == m, s, idx)
                part[d, yy, cc] = lax.dot_general(
                    adj[idx], back_ref[...], (((0,), (0,)), ((), ())), preferred_element_type=F32
                ).astype(BF16)
        rc_copy(d).start()
        return carry

    lax.fori_loop(0, n_z, transposed, 0)

    gw_c.wait_recv()
    gwc[...] += gwt[g_row(rep, c), :]
    gw_y = rcopy(gwc.at[:, g_col(1 - y)], gwy, gw_s.at[1], gw_r.at[1], dev(z, 1 - y, c))
    gw_y.start()

    def add_core(d, carry):
        rc_copy(d).wait_recv()
        for yy in range(n_y):
            part[d, yy, c] = (part[d, yy, c].astype(F32) + rc[d, yy].astype(F32)).astype(BF16)
        return carry

    def yb_copy(d):
        return rcopy(part.at[d, 1 - y, c, ROWS_B], ryb.at[d], rs_s.at[3, 0, d], rs_r.at[3, 0, d], dev(z, 1 - y, c))

    def add_core_send(d, carry):
        add_core(d, carry)
        yb_copy(d).start()
        return carry

    lax.fori_loop(0, n_z, add_core_send, 0)

    def rs_dest(d, t):
        return z - n_z + 1 + t if d == 0 else z + n_z - 1 - t

    def rs_send_ok(d, t):
        return z - n_z + 1 + t >= 0 if d == 0 else z + n_z - 1 - t <= n_z - 1

    def rs_send_ok2(d, t):
        dst = rs_dest(d, t)
        return (dst >= 0) & (z >= 1) if d == 0 else (dst <= n_z - 1) & (z <= n_z - 2)

    def rs_recv_ok(d, t):
        w = z + 1 if d == 0 else z - 1
        dst = w - n_z + 1 + t if d == 0 else w + n_z - 1 - t
        return (w <= n_z - 1) & (dst >= 0) if d == 0 else (w >= 0) & (dst <= n_z - 1)

    def rs_recv_dest(d, t):
        return z + 2 - n_z + t if d == 0 else z + n_z - 2 - t

    def za_copy(d, t):
        return rcopy(
            part.at[rs_dest(d, t), :, c, ROWS_A], rza.at[d, t],
            rs_s.at[0, d, t], rs_r.at[0, d, t], dev(z - 1 if d == 0 else z + 1, y, c),
        )

    def zb_copy(d, t):
        return rcopy(
            part.at[rs_dest(d, t), y, c, ROWS_B], rzb.at[d, t],
            rs_s.at[1, d, t], rs_r.at[1, d, t], dev(z - 1 if d == 0 else z + 1, y, c),
        )

    def za_got(d, t):
        return rcopy(
            part.at[z, :, c, ROWS_A], rza.at[d, t],
            rs_s.at[0, d, t], rs_r.at[0, d, t], dev(z, y, 1 - c),
        )

    def zb_got(d, t):
        return rcopy(
            part.at[z, y, c, ROWS_B], rzb.at[d, t],
            rs_s.at[1, d, t], rs_r.at[1, d, t], dev(z, y, 1 - c),
        )

    def take_a(d, t):
        za_got(d, t).wait_recv()
        dst = rs_recv_dest(d, t)
        for yy in range(n_y):
            part[dst, yy, c, ROWS_A] = (
                part[dst, yy, c, ROWS_A].astype(F32) + rza[d, t, yy].astype(F32)
            ).astype(BF16)

    def take_b(d, t):
        zb_got(d, t).wait_recv()
        dst = rs_recv_dest(d, t)
        part[dst, y, c, ROWS_B] = (
            part[dst, y, c, ROWS_B].astype(F32) + rzb[d, t].astype(F32)
        ).astype(BF16)

    for d in range(2):
        pl.when(rs_send_ok2(d, 0))(za_copy(d, 0).start)

    gw_y.wait_recv()
    gwz[z] = gwc[:, g_col(y)] + gwy[...]

    def gz_copy(j, got=False):
        other = (z + n_z - j if got else z + j) % n_z
        blk = gwz.at[other if got else z]
        return rcopy(blk, blk, gwz_s.at[j - 1], gwz_r.at[j - 1], dev(other, y, c))

    for j in range(1, n_z):
        gz_copy(j).start()

    def take_yb(d, carry):
        yb_copy(d).wait_recv()
        part[d, y, c, ROWS_B] = (
            part[d, y, c, ROWS_B].astype(F32) + ryb[d].astype(F32)
        ).astype(BF16)
        return carry

    lax.fori_loop(0, n_z, take_yb, 0)
    for t in range(n_z - 1):
        for d in range(2):
            pl.when(rs_send_ok2(d, t))(zb_copy(d, t).start)
        for d in range(2):
            pl.when(rs_recv_ok(d, t))(functools.partial(take_a, d, t))
            if t + 1 < n_z - 1:
                pl.when(rs_send_ok2(d, t + 1))(za_copy(d, t + 1).start)
        for d in range(2):
            pl.when(rs_recv_ok(d, t))(functools.partial(take_b, d, t))
        if t == 0:
            for j in range(1, n_z):
                gz_copy(j, True).wait_recv()
            gsum = gwz[0]
            for j in range(1, n_z):
                gsum = gsum + gwz[j]
            gw_ref[g_row(rep, c), g_col(y)] = gsum * scale
            mine = gw_ref.at[g_row(rep, c), g_col(y)]
            g_y = rcopy(mine, mine, gw_s.at[2], gw_r.at[2], dev(z, 1 - y, c))
            g_y.start()

        if t == min(1, n_z - 2):
            theirs = gw_ref.at[g_row(rep, c), g_col(1 - y)]
            rcopy(theirs, theirs, gw_s.at[2], gw_r.at[2], dev(z, 1 - y, c)).wait_recv()
            strip = gw_ref.at[g_row(rep, c)]
            g_c = rcopy(strip, strip, gw_s.at[3], gw_r.at[3], dev(z, y, 1 - c))
            g_c.start()
    ya = rcopy(part.at[z, 1 - y, c, ROWS_A], rya, rs_s.at[2, 0, 0], rs_r.at[2, 0, 0], dev(z, 1 - y, c))
    ya.start()

    strip2 = gw_ref.at[g_row(rep, 1 - c)]
    rcopy(strip2, strip2, gw_s.at[3], gw_r.at[3], dev(z, y, 1 - c)).wait_recv()

    def gx_copy(j, got=False):
        other = (rep + n_rep - j if got else rep + j) % n_rep
        rows = gw_ref.shape[0] // n_rep
        blk = gw_ref.at[pl.ds(pl.multiple_of((other if got else rep) * rows, rows), rows)]
        return rcopy(blk, blk, gwx_s.at[j - 1], gwx_r.at[j - 1], (other, me))

    for j in range(1, n_rep):
        gx_copy(j).start()
    ya.wait_recv()
    xo[rep, ROWS_B] = part[z, y, c, ROWS_B]
    xo[rep, ROWS_A] = (part[z, y, c, ROWS_A].astype(F32) + rya[...].astype(F32)).astype(BF16)
    for j in range(1, n_rep):
        x_copy(xo, 1, j).start()

    for j in range(1, n_rep):
        x_copy(xo, 1, j, True).wait_recv()
    out = back_ref[...].astype(F32)
    for r in range(n_rep):
        out = out + xo[r].astype(F32)
    gx_ref[...] = out
    for j in range(1, n_rep):
        gx_copy(j, True).wait_recv()

    store.wait()
    own_y(ROWS_A, 0).wait_send()
    own_y(ROWS_B, 1).wait_send()
    for kind in range(2):
        sib(kind, z, 0).wait_send()
    for t in range(n_z - 1):
        for d in range(2):
            pl.when(send_ok(d, t))(a_z(d, t).wait_send)
            pl.when(send_ok(d, t))(b_z(d, t).wait_send)
            pl.when(recv_ok(d, t))(b_y(d, t).wait_send)
            for kind in range(2):
                pl.when(recv_ok(d, t))(sib(kind, origin(d, t), 1 + 2 * t + d).wait_send)
            pl.when(rs_send_ok2(d, t))(za_copy(d, t).wait_send)
            pl.when(rs_send_ok2(d, t))(zb_copy(d, t).wait_send)
    for d in range(n_z):
        rc_copy(d).wait_send()
        yb_copy(d).wait_send()
    ya.wait_send()
    for j in range(1, n_rep):
        x_copy(xg, 0, j).wait_send()
        x_copy(xo, 1, j).wait_send()
        gx_copy(j).wait_send()
    for j in range(1, n_z):
        gz_copy(j).wait_send()
    for g in (gw_c, gw_y, g_y, g_c):
        g.wait_send()


def finish_kernel(a, b, c, a_out, b_out, c_out):
    for src, dst in ((a, a_out), (b, b_out), (c, c_out)):
        dst[...] = src[...]


def per_device(
    n_rep, n_grp,
    features, weight, bias_row, cotangent, tile_vals, row_block, col_block, counts, owner_map
):
    side = tile_vals.shape[-1]
    n_sections = tile_vals.shape[2]
    rows, width = features.shape
    hid = weight.shape[1]
    n_c, n_y = 2, 2
    n_z = n_grp // (n_c * n_y)
    half = rows // 2
    vmem = pl.BlockSpec(memory_space=pltpu.VMEM)
    dma = pltpu.SemaphoreType.DMA
    g_rows = width // (n_rep * n_c)
    g_cols = hid // n_y
    smem = pl.BlockSpec(memory_space=pltpu.SMEM)
    hbm = pl.BlockSpec(memory_space=pl.ANY)
    outs = pl.pallas_call(
        functools.partial(main_kernel, n_rep, n_z, n_y, n_c, float((rows * n_grp) ** (-0.5))),
        out_shape=(
            jax.ShapeDtypeStruct((rows, hid), BF16),
            jax.ShapeDtypeStruct((width, hid), F32),
            jax.ShapeDtypeStruct((rows, width), F32),
        ),
        in_specs=[smem, smem, smem, smem, hbm, hbm, vmem, hbm, hbm],
        out_specs=(hbm, vmem, vmem),
        scratch_shapes=[
            pltpu.VMEM(tile_vals.shape[2:], BF16),
            pltpu.VMEM((rows, width), BF16),
            pltpu.VMEM((width, hid), BF16),
            pltpu.VMEM((rows, hid), BF16),
            pltpu.VMEM((rows, hid), BF16),
            pltpu.VMEM((n_sections + 1, rows, rows), BF16),
            pltpu.VMEM((n_z, n_y, n_c, rows, width), BF16),
            pltpu.VMEM((n_z, n_y, n_c, rows, width), BF16),
            pltpu.VMEM((n_z, n_y, rows, width), BF16),
            pltpu.VMEM((2, n_z - 1, n_y, half, width), BF16),
            pltpu.VMEM((2, n_z - 1, half, width), BF16),
            pltpu.VMEM((half, width), BF16),
            pltpu.VMEM((n_z, half, width), BF16),
            pltpu.VMEM((n_rep, rows, width), BF16),
            pltpu.VMEM((n_rep, rows, width), BF16),
            pltpu.VMEM((width, hid), F32),
            pltpu.VMEM((g_rows, hid), F32),
            pltpu.VMEM((g_rows, g_cols), F32),
            pltpu.VMEM((n_z, g_rows, g_cols), F32),
            pltpu.VMEM((rows, width), BF16),
            dma((n_sections,)), dma((4,)),
            dma((4, 2, n_z)), dma((4, 2, n_z)),
            dma((2, 2 * n_z)), dma((2, 2 * n_z)),
            dma((n_z,)), dma((n_z,)),
            dma((4, 2, n_z)), dma((4, 2, n_z)),
            dma((2, n_rep)), dma((2, n_rep)),
            dma((4,)), dma((4,)),
            dma((n_z,)), dma((n_z,)),
            dma((n_rep,)), dma((n_rep,)),
        ],
        compiler_params=pltpu.CompilerParams(
            collective_id=0, has_side_effects=True, vmem_limit_bytes=56 * 1024 * 1024
        ),
    )(owner_map, row_block, col_block, counts, features, weight, bias_row[None, :], cotangent, tile_vals)
    return pl.pallas_call(
        finish_kernel,
        out_shape=tuple(jax.ShapeDtypeStruct(o.shape, o.dtype) for o in outs),
        in_specs=[vmem] * 3,
        out_specs=(vmem,) * 3,
    )(*outs)


def solution(mesh):
    in_specs = (
        P("grp", None),
        P(),
        P(),
        P("grp", None),
        P("rep", "grp", None, None, None, None),
        P("rep", "grp", None, None),
        P("rep", "grp", None, None),
        P("rep", "grp", None),
        P(),
    )
    out_specs = (P("grp", None), P(), P("grp", None))
    return jax.shard_map(
        functools.partial(per_device, mesh.shape["rep"], mesh.shape["grp"]),
        mesh=mesh, in_specs=in_specs, out_specs=out_specs, check_vma=False,
    )
```

```python
import functools

import jax
import jax.numpy as jnp
from jax import lax
from jax.experimental import pallas as pl
from jax.experimental.pallas import tpu as pltpu
from jax.sharding import PartitionSpec as P

BF16 = jnp.bfloat16
F32 = jnp.float32


def main_kernel(
    n_rep, n_z, n_y, n_c, scale,
    owner_ref, row_ref, col_ref, count_ref, feat_hbm, weight_hbm, bias_ref, cot_hbm, tiles_hbm,
    hidden_hbm, gw_ref, gx_ref,
    tiles, feat_ref, weight_ref, cot_ref, hidden_ref, adj, feats, part, rc, rza, rzb, rya, ryb, xg, xo, gwt, gwc, gwy, gwz, back_ref,
    tile_sem, in_sem, ag_s, ag_r, sib_s, sib_r, rc_s, rc_r, rs_s, rs_r, x_s, x_r, gw_s, gw_r, gwz_s, gwz_r, gwx_s, gwx_r,
):
    rep = lax.axis_index("rep")
    me = lax.axis_index("grp")
    z = me // (n_y * n_c)
    y = (me // n_c) % n_y
    c = me % n_c
    cut = rya.shape[0]
    short = n_z == 4
    n_sections, n_slots, side, _ = tiles.shape
    n_blocks = feat_ref.shape[0] // side
    ROWS_A, ROWS_B = pl.ds(0, cut), pl.ds(cut, feat_ref.shape[0] - cut)

    def dev(zz, yy, cc):
        return (rep, (zz * n_y + yy) * n_c + cc)

    def rcopy(src, dst, s_sem, r_sem, target):
        return pltpu.make_async_remote_copy(
            src_ref=src, dst_ref=dst, send_sem=s_sem, recv_sem=r_sem,
            device_id=target, device_id_type=pl.DeviceIdType.MESH,
        )

    loads = [
        pltpu.make_async_copy(feat_hbm, feats.at[z, y, c], in_sem.at[0]),
        pltpu.make_async_copy(feat_hbm, feat_ref, in_sem.at[1]),
        pltpu.make_async_copy(weight_hbm, weight_ref, in_sem.at[2]),
        pltpu.make_async_copy(cot_hbm, cot_ref, in_sem.at[3]),
    ]
    loads[0].start()

    barrier = pltpu.get_barrier_semaphore()

    def greet(target):
        pl.semaphore_signal(barrier, inc=1, device_id=target, device_id_type=pl.DeviceIdType.MESH)

    greet(dev(z, y, 1 - c))
    greet(dev(z, 1 - y, c))
    for j in range(1, n_z):
        greet(dev((z + j) % n_z, y, c))
    for j in range(1, n_rep):
        greet(((rep + j) % n_rep, me))
    tile_loads = [
        pltpu.make_async_copy(tiles_hbm.at[0, 0, s], tiles.at[s], tile_sem.at[s])
        for s in range(n_sections)
    ]
    for s in range(n_sections):
        tile_loads[s].start()
    for load in loads[1:]:
        load.start()
    adj[n_sections] = jnp.zeros_like(adj[n_sections])
    pl.semaphore_wait(barrier, 2 + n_z - 1 + n_rep - 1)
    loads[0].wait()

    part_rows = side // 2

    def build(s):
        tile_loads[s].wait()
        place = [
            jnp.where(
                k < count_ref[0, 0, s], row_ref[0, 0, s, k] * n_blocks + col_ref[0, 0, s, k], -1
            )
            for k in range(n_slots)
        ]

        def column(j, carry):
            cols = pl.ds(pl.multiple_of(j * side, side), side)
            for h in range(2):
                sums = [jnp.zeros((part_rows, side), F32)] * n_blocks
                for k in range(n_slots):
                    tile = tiles[s, k, h * part_rows : (h + 1) * part_rows, :].astype(F32)
                    for i in range(n_blocks):
                        pick = jnp.where(place[k] == i * n_blocks + j, 1.0, 0.0).astype(F32)
                        sums[i] = sums[i] + pick * tile
                for i in range(n_blocks):
                    lo = i * side + h * part_rows
                    adj[s, lo : lo + part_rows, cols] = sums[i].astype(BF16)
            return carry

        lax.fori_loop(0, n_blocks, column, 0)

    todo = list(range(n_sections))

    def build_next():
        if todo:
            build(todo.pop(0))

    def a_z(d, t, jump=False):
        src = z if jump else z - t if d == 0 else z + t
        blk = feats.at[src, :, c, ROWS_A]
        step = 2 if jump else 1
        return rcopy(blk, blk, ag_s.at[0, d, t], ag_r.at[0, d, t], dev(z + step if d == 0 else z - step, y, c))

    def b_z(d, t, jump=False):
        src = z if jump else z - t if d == 0 else z + t
        blk = feats.at[src, y, c, ROWS_B]
        step = 2 if jump else 1
        return rcopy(blk, blk, ag_s.at[1, d, t], ag_r.at[1, d, t], dev(z + step if d == 0 else z - step, y, c))

    def jump_ok(d):
        return z == 0 if d == 0 else z == n_z - 1

    def send_ok(d, t):
        if short and t == 1:
            return z == 2 if d == 0 else z == 1
        return (z - t >= 0) & (z + 1 < n_z) if d == 0 else (z + t < n_z) & (z >= 1)

    def recv_ok(d, t):
        return z - 1 - t >= 0 if d == 0 else z + 1 + t < n_z

    def origin(d, t):
        return z - 1 - t if d == 0 else z + 1 + t

    def arrived(kind, d, t):
        src = origin(d, t)
        blk = feats.at[src, :, c, ROWS_A] if kind == 0 else feats.at[src, y, c, ROWS_B]
        if kind == 2:
            blk = feats.at[src, 1 - y, c, ROWS_B]
        return rcopy(blk, blk, ag_s.at[kind, d, t], ag_r.at[kind, d, t], dev(z, y, 1 - c))

    def b_y(d, t):
        src = origin(d, t)
        blk = feats.at[src, y, c, ROWS_B]
        return rcopy(blk, blk, ag_s.at[2, d, t], ag_r.at[2, d, t], dev(z, 1 - y, c))

    def sib(kind, src, i, got=False):
        blk = feats.at[src, :, 1 - c if got else c, ROWS_A if kind == 0 else ROWS_B]
        return rcopy(blk, blk, sib_s.at[kind, i], sib_r.at[kind, i], dev(z, y, 1 - c))

    def own_y(rows, i, got=False):
        blk = feats.at[z, 1 - y if got else y, c, rows]
        return rcopy(blk, blk, ag_s.at[3, i, 0], ag_r.at[3, i, 0], dev(z, 1 - y, c))

    own_y(ROWS_A, 0).start()
    for d in range(2):
        pl.when(send_ok(d, 0))(b_z(d, 0).start)
        if short:
            pl.when(jump_ok(d))(b_z(d, 1, True).start)
    own_y(ROWS_B, 1).start()
    build_next()
    own_y(ROWS_A, 0, True).wait_recv()
    for d in range(2):
        pl.when(send_ok(d, 0))(a_z(d, 0).start)
        if short:
            pl.when(jump_ok(d))(a_z(d, 1, True).start)
    sib(0, z, 0).start()
    build_next()
    own_y(ROWS_B, 1, True).wait_recv()
    sib(1, z, 0).start()
    for t in range(n_z - 1):
        build_next()
        for d in range(2):
            pl.when(recv_ok(d, t))(arrived(1, d, t).wait_recv)
            if t + 1 < n_z - 1:
                pl.when(send_ok(d, t + 1))(b_z(d, t + 1).start)
            pl.when(recv_ok(d, t))(b_y(d, t).start)
        build_next()
        for d in range(2):
            pl.when(recv_ok(d, t))(arrived(0, d, t).wait_recv)
            if t + 1 < n_z - 1:
                pl.when(send_ok(d, t + 1))(a_z(d, t + 1).start)
            pl.when(recv_ok(d, t))(sib(0, origin(d, t), 1 + 2 * t + d).start)
        for d in range(2):
            pl.when(recv_ok(d, t))(arrived(2, d, t).wait_recv)
            pl.when(recv_ok(d, t))(sib(1, origin(d, t), 1 + 2 * t + d).start)
    while todo:
        build_next()
    for kind in range(2):
        sib(kind, z, 0, True).wait_recv()
    for t in range(n_z - 1):
        for d in range(2):
            for kind in range(2):
                pl.when(recv_ok(d, t))(sib(kind, origin(d, t), 1 + 2 * t + d, True).wait_recv)
    for load in loads[1:]:
        load.wait()

    def forward(s, total):
        o = owner_ref[rep * n_sections + s]
        f = feats[lax.div(o, n_y * n_c), lax.rem(lax.div(o, n_c), n_y), lax.rem(o, n_c)]
        return total + jnp.dot(adj[s], f, preferred_element_type=F32)

    total = lax.fori_loop(0, n_sections, forward, jnp.zeros(feat_ref.shape, F32))
    xg[rep] = total.astype(BF16)

    def x_copy(buf, kind, j, got=False):
        other = (rep + n_rep - j if got else rep + j) % n_rep
        blk = buf.at[other if got else rep]
        return rcopy(blk, blk, x_s.at[kind, j - 1], x_r.at[kind, j - 1], (other, me))

    def xo_copy(j, rows, kind, got=False):
        other = (rep + n_rep - j if got else rep + j) % n_rep
        blk = xo.at[other if got else rep, rows]
        return rcopy(blk, blk, x_s.at[kind, j - 1], x_r.at[kind, j - 1], (other, me))

    for j in range(1, n_rep):
        x_copy(xg, 0, j).start()
    for j in range(1, n_rep):
        x_copy(xg, 0, j, True).wait_recv()
    agg = feat_ref[...].astype(F32)
    for r in range(n_rep):
        agg = agg + xg[r].astype(F32)
    agg_rows = agg.astype(BF16)
    pre = jnp.dot(agg_rows, weight_ref[...], preferred_element_type=F32) + bias_ref[...]
    sig = jax.nn.sigmoid(pre)
    hidden_ref[...] = (pre * sig).astype(BF16)
    store = pltpu.make_async_copy(hidden_ref, hidden_hbm, in_sem.at[0])
    store.start()
    grad_pre = (cot_ref[...].astype(F32) * sig * (1.0 + pre * (1.0 - sig))).astype(BF16)
    back = lax.dot_general(
        grad_pre, weight_ref[...], (((1,), (1,)), ((), ())), preferred_element_type=F32
    ).astype(BF16)
    back_ref[...] = back
    gwt[...] = lax.dot_general(agg_rows, grad_pre, (((0,), (0,)), ((), ())), preferred_element_type=F32)

    g_rows = gw_ref.shape[0] // (n_rep * n_c)
    g_cols = gw_ref.shape[1] // n_y

    def g_row(r, cc):
        return pl.ds(pl.multiple_of((r * n_c + cc) * g_rows, g_rows), g_rows)

    def g_col(yy):
        return pl.ds(pl.multiple_of(yy * g_cols, g_cols), g_cols)

    gw_c = rcopy(gwt.at[g_row(rep, 1 - c)], gwc, gw_s.at[0], gw_r.at[0], dev(z, y, 1 - c))
    gw_c.start()

    def rc_copy(d):
        return rcopy(part.at[d, :, 1 - c], rc.at[d], rc_s.at[d], rc_r.at[d], dev(z, y, 1 - c))

    def transposed(d, carry):
        for yy in range(n_y):
            for cc in range(n_c):
                m = (d * n_y + yy) * n_c + cc
                idx = jnp.int32(n_sections)
                for s in range(n_sections):
                    idx = jnp.where(owner_ref[rep * n_sections + s] == m, s, idx)
                part[d, yy, cc] = lax.dot_general(
                    adj[idx], back_ref[...], (((0,), (0,)), ((), ())), preferred_element_type=F32
                ).astype(BF16)
        rc_copy(d).start()
        return carry

    lax.fori_loop(0, n_z, transposed, 0)

    gw_c.wait_recv()
    gwc[...] += gwt[g_row(rep, c), :]
    gw_y = rcopy(gwc.at[:, g_col(1 - y)], gwy, gw_s.at[1], gw_r.at[1], dev(z, 1 - y, c))
    gw_y.start()

    def add_core(d, carry):
        rc_copy(d).wait_recv()
        for yy in range(n_y):
            part[d, yy, c] = (part[d, yy, c].astype(F32) + rc[d, yy].astype(F32)).astype(BF16)
        return carry

    def yb_copy(d):
        return rcopy(part.at[d, 1 - y, c, ROWS_B], ryb.at[d], rs_s.at[3, 0, d], rs_r.at[3, 0, d], dev(z, 1 - y, c))

    def rs_dest(d, t):
        return z - n_z + 1 + t if d == 0 else z + n_z - 1 - t

    def rs_send_ok2(d, t):
        dst = rs_dest(d, t)
        return (dst >= 0) & (z >= 1) if d == 0 else (dst <= n_z - 1) & (z <= n_z - 2)

    def at_end(d):
        return z == n_z - 1 if d == 0 else z == 0

    def at_second(d):
        return z == n_z - 2 if d == 0 else z == 1

    def at_third(d):
        return z == 1 if d == 0 else z == n_z - 2

    def at_far(d):
        return z == 0 if d == 0 else z == n_z - 1

    def rs_target(d, t):
        step = jnp.where(at_second(d), 2, 1) if short and t == 1 else 1
        return dev(z - step if d == 0 else z + step, y, c)

    def rs_recv_ok(d, t):
        if short and t == 1:
            return at_second(d) | at_far(d)
        w = z + 1 if d == 0 else z - 1
        dst = w - n_z + 1 + t if d == 0 else w + n_z - 1 - t
        return (w <= n_z - 1) & (dst >= 0) if d == 0 else (w >= 0) & (dst <= n_z - 1)

    def rs_recv_dest(d, t):
        dst = z + 2 - n_z + t if d == 0 else z + n_z - 2 - t
        return jnp.where(at_far(d), z, dst) if short and t == 1 else dst

    def za_copy(d, t):
        return rcopy(
            part.at[rs_dest(d, t), :, c, ROWS_A], rza.at[d, t],
            rs_s.at[0, d, t], rs_r.at[0, d, t], rs_target(d, t),
        )

    def zb_copy(d, t):
        return rcopy(
            part.at[rs_dest(d, t), y, c, ROWS_B], rzb.at[d, t],
            rs_s.at[1, d, t], rs_r.at[1, d, t], rs_target(d, t),
        )

    def za_got(d, t):
        return rcopy(
            part.at[z, :, c, ROWS_A], rza.at[d, t],
            rs_s.at[0, d, t], rs_r.at[0, d, t], dev(z, y, 1 - c),
        )

    def zb_got(d, t):
        return rcopy(
            part.at[z, y, c, ROWS_B], rzb.at[d, t],
            rs_s.at[1, d, t], rs_r.at[1, d, t], dev(z, y, 1 - c),
        )

    def take_a(d, t):
        za_got(d, t).wait_recv()
        dst = rs_recv_dest(d, t)
        for yy in range(n_y):
            part[dst, yy, c, ROWS_A] = (
                part[dst, yy, c, ROWS_A].astype(F32) + rza[d, t, yy].astype(F32)
            ).astype(BF16)

    def take_b(d, t):
        zb_got(d, t).wait_recv()
        dst = rs_recv_dest(d, t)
        part[dst, y, c, ROWS_B] = (
            part[dst, y, c, ROWS_B].astype(F32) + rzb[d, t].astype(F32)
        ).astype(BF16)

    def first_sends(copy_of, dst):
        for d in range(2):
            t = dst if d == 0 else n_z - 1 - dst
            if t < n_z - 1 and (short or t == 0):
                pl.when(at_end(d))(copy_of(d, t).start)
            if short and t == 0:
                pl.when(at_third(d))(copy_of(d, n_z - 2).start)

    def later_send(copy_of, d, t):
        pl.when(at_second(d) if short else rs_send_ok2(d, t))(copy_of(d, t).start)

    for dst in range(n_z):
        add_core(dst, 0)
        yb_copy(dst).start()
        first_sends(za_copy, dst)

    gw_y.wait_recv()
    gwz[z] = gwc[:, g_col(y)] + gwy[...]

    def gz_copy(j, got=False):
        other = (z + n_z - j if got else z + j) % n_z
        blk = gwz.at[other if got else z]
        return rcopy(blk, blk, gwz_s.at[j - 1], gwz_r.at[j - 1], dev(other, y, c))

    for j in range(1, n_z):
        gz_copy(j).start()

    def take_yb(d, carry):
        yb_copy(d).wait_recv()
        part[d, y, c, ROWS_B] = (
            part[d, y, c, ROWS_B].astype(F32) + ryb[d].astype(F32)
        ).astype(BF16)
        return carry

    def take_all(take, copy_of, t):
        for d in range(2):
            pl.when(rs_recv_ok(d, t))(functools.partial(take, d, t))
            if t + 1 < n_z - 1:
                later_send(copy_of, d, t + 1)

    take_all(take_a, za_copy, 0)
    for dst in range(n_z):
        take_yb(dst, 0)
        first_sends(zb_copy, dst)
    for t in range(1, n_z - 1):
        take_all(take_a, za_copy, t)
        if t == n_z - 2:
            ya = rcopy(part.at[z, 1 - y, c, ROWS_A], rya, rs_s.at[2, 0, 0], rs_r.at[2, 0, 0], dev(z, 1 - y, c))
            ya.start()
        take_all(take_b, zb_copy, t - 1)
        if t == 1:
            for j in range(1, n_z):
                gz_copy(j, True).wait_recv()
            gsum = gwz[0]
            for j in range(1, n_z):
                gsum = gsum + gwz[j]
            gw_ref[g_row(rep, c), g_col(y)] = gsum * scale
            mine = gw_ref.at[g_row(rep, c), g_col(y)]
            g_y = rcopy(mine, mine, gw_s.at[2], gw_r.at[2], dev(z, 1 - y, c))
            g_y.start()

    take_all(take_b, zb_copy, n_z - 2)
    xo[rep, ROWS_B] = part[z, y, c, ROWS_B]
    for j in range(1, n_rep):
        xo_copy(j, ROWS_B, 1).start()
    theirs = gw_ref.at[g_row(rep, c), g_col(1 - y)]
    rcopy(theirs, theirs, gw_s.at[2], gw_r.at[2], dev(z, 1 - y, c)).wait_recv()
    strip = gw_ref.at[g_row(rep, c)]
    g_c = rcopy(strip, strip, gw_s.at[3], gw_r.at[3], dev(z, y, 1 - c))
    g_c.start()

    strip2 = gw_ref.at[g_row(rep, 1 - c)]
    rcopy(strip2, strip2, gw_s.at[3], gw_r.at[3], dev(z, y, 1 - c)).wait_recv()

    def gx_copy(j, got=False):
        other = (rep + n_rep - j if got else rep + j) % n_rep
        rows = gw_ref.shape[0] // n_rep
        blk = gw_ref.at[pl.ds(pl.multiple_of((other if got else rep) * rows, rows), rows)]
        return rcopy(blk, blk, gwx_s.at[j - 1], gwx_r.at[j - 1], (other, me))

    for j in range(1, n_rep):
        gx_copy(j).start()
    ya.wait_recv()
    xo[rep, ROWS_A] = (part[z, y, c, ROWS_A].astype(F32) + rya[...].astype(F32)).astype(BF16)
    for j in range(1, n_rep):
        xo_copy(j, ROWS_A, 2).start()

    for j in range(1, n_rep):
        xo_copy(j, ROWS_B, 1, True).wait_recv()
        xo_copy(j, ROWS_A, 2, True).wait_recv()
    out = back_ref[...].astype(F32)
    for r in range(n_rep):
        out = out + xo[r].astype(F32)
    gx_ref[...] = out
    for j in range(1, n_rep):
        gx_copy(j, True).wait_recv()

    store.wait()
    own_y(ROWS_A, 0).wait_send()
    own_y(ROWS_B, 1).wait_send()
    for kind in range(2):
        sib(kind, z, 0).wait_send()
    for t in range(n_z - 1):
        for d in range(2):
            pl.when(send_ok(d, t))(a_z(d, t).wait_send)
            pl.when(send_ok(d, t))(b_z(d, t).wait_send)
            pl.when(recv_ok(d, t))(b_y(d, t).wait_send)
            for kind in range(2):
                pl.when(recv_ok(d, t))(sib(kind, origin(d, t), 1 + 2 * t + d).wait_send)
            pl.when(rs_send_ok2(d, t))(za_copy(d, t).wait_send)
            pl.when(rs_send_ok2(d, t))(zb_copy(d, t).wait_send)
    if short:
        for d in range(2):
            pl.when(jump_ok(d))(a_z(d, 1, True).wait_send)
            pl.when(jump_ok(d))(b_z(d, 1, True).wait_send)
    for d in range(n_z):
        rc_copy(d).wait_send()
        yb_copy(d).wait_send()
    ya.wait_send()
    for j in range(1, n_rep):
        x_copy(xg, 0, j).wait_send()
        xo_copy(j, ROWS_B, 1).wait_send()
        xo_copy(j, ROWS_A, 2).wait_send()
        gx_copy(j).wait_send()
    for j in range(1, n_z):
        gz_copy(j).wait_send()
    for g in (gw_c, gw_y, g_y, g_c):
        g.wait_send()


def finish_kernel(a, b, c, a_out, b_out, c_out):
    for src, dst in ((a, a_out), (b, b_out), (c, c_out)):
        dst[...] = src[...]


def per_device(
    n_rep, n_grp,
    features, weight, bias_row, cotangent, tile_vals, row_block, col_block, counts, owner_map
):
    side = tile_vals.shape[-1]
    n_sections = tile_vals.shape[2]
    rows, width = features.shape
    hid = weight.shape[1]
    n_c, n_y = 2, 2
    n_z = n_grp // (n_c * n_y)
    cut = rows // 4
    vmem = pl.BlockSpec(memory_space=pltpu.VMEM)
    dma = pltpu.SemaphoreType.DMA
    g_rows = width // (n_rep * n_c)
    g_cols = hid // n_y
    smem = pl.BlockSpec(memory_space=pltpu.SMEM)
    hbm = pl.BlockSpec(memory_space=pl.ANY)
    outs = pl.pallas_call(
        functools.partial(main_kernel, n_rep, n_z, n_y, n_c, float((rows * n_grp) ** (-0.5))),
        out_shape=(
            jax.ShapeDtypeStruct((rows, hid), BF16),
            jax.ShapeDtypeStruct((width, hid), F32),
            jax.ShapeDtypeStruct((rows, width), F32),
        ),
        in_specs=[smem, smem, smem, smem, hbm, hbm, vmem, hbm, hbm],
        out_specs=(hbm, vmem, vmem),
        scratch_shapes=[
            pltpu.VMEM(tile_vals.shape[2:], BF16),
            pltpu.VMEM((rows, width), BF16),
            pltpu.VMEM((width, hid), BF16),
            pltpu.VMEM((rows, hid), BF16),
            pltpu.VMEM((rows, hid), BF16),
            pltpu.VMEM((n_sections + 1, rows, rows), BF16),
            pltpu.VMEM((n_z, n_y, n_c, rows, width), BF16),
            pltpu.VMEM((n_z, n_y, n_c, rows, width), BF16),
            pltpu.VMEM((n_z, n_y, rows, width), BF16),
            pltpu.VMEM((2, n_z - 1, n_y, cut, width), BF16),
            pltpu.VMEM((2, n_z - 1, rows - cut, width), BF16),
            pltpu.VMEM((cut, width), BF16),
            pltpu.VMEM((n_z, rows - cut, width), BF16),
            pltpu.VMEM((n_rep, rows, width), BF16),
            pltpu.VMEM((n_rep, rows, width), BF16),
            pltpu.VMEM((width, hid), F32),
            pltpu.VMEM((g_rows, hid), F32),
            pltpu.VMEM((g_rows, g_cols), F32),
            pltpu.VMEM((n_z, g_rows, g_cols), F32),
            pltpu.VMEM((rows, width), BF16),
            dma((n_sections,)), dma((4,)),
            dma((4, 2, n_z)), dma((4, 2, n_z)),
            dma((2, 2 * n_z)), dma((2, 2 * n_z)),
            dma((n_z,)), dma((n_z,)),
            dma((4, 2, n_z)), dma((4, 2, n_z)),
            dma((3, n_rep)), dma((3, n_rep)),
            dma((4,)), dma((4,)),
            dma((n_z,)), dma((n_z,)),
            dma((n_rep,)), dma((n_rep,)),
        ],
        compiler_params=pltpu.CompilerParams(
            collective_id=0, has_side_effects=True, vmem_limit_bytes=56 * 1024 * 1024
        ),
    )(owner_map, row_block, col_block, counts, features, weight, bias_row[None, :], cotangent, tile_vals)
    return pl.pallas_call(
        finish_kernel,
        out_shape=tuple(jax.ShapeDtypeStruct(o.shape, o.dtype) for o in outs),
        in_specs=[vmem] * 3,
        out_specs=(vmem,) * 3,
    )(*outs)


def solution(mesh):
    in_specs = (
        P("grp", None),
        P(),
        P(),
        P("grp", None),
        P("rep", "grp", None, None, None, None),
        P("rep", "grp", None, None),
        P("rep", "grp", None, None),
        P("rep", "grp", None),
        P(),
    )
    out_specs = (P("grp", None), P(), P("grp", None))
    return jax.shard_map(
        functools.partial(per_device, mesh.shape["rep"], mesh.shape["grp"]),
        mesh=mesh, in_specs=in_specs, out_specs=out_specs, check_vma=False,
    )
```
